256 devices in a mesh: tm: 8 (over z), space: 32 (over x, y, core).
Axes of the slice: x: 4, y: 4, z: 8, core: 2. Of those that a mesh axis runs over, the one named last changes fastest.
Arguments:
- snapshots: float32 [4096, 32768], P('tm', 'space')
- weights: float32 [32768], P('space'), may hold values from 0.25 to 4
Outputs:
- modes: float32 [64, 2, 4, 32768], P('tm', None, None, 'space')
- cross_spectra: float32 [64, 2, 31, 31], P('tm')
The draws below stay inside these ranges and needn't reach their ends.
All inputs are finite; a program needn't handle non-finite values.
Results may differ from the reference program's by a relative error of at most 0.00014.
Values sent between devices are 32-bit elements; how exact they have to be, the bound alone decides.
A program may use at most 128 MiB of HBM per device.

```python
import math
import jax
import jax.numpy as jnp
from jax import lax

NFFT = 256
STRIDE = 128
NFREQ = 64
NMODE = 4
NB = 31
TIME = 4096
POINTS = 32768


def draw_snapshots(key, part):
    key = jax.random.fold_in(key, 11)
    keys = jax.random.split(key, 5)
    ranks = 8
    amps = jax.random.truncated_normal(keys[0], -4.0, 4.0, (TIME, ranks), jnp.float32)
    shapes = jax.random.truncated_normal(keys[1], -4.0, 4.0, (ranks, POINTS), jnp.float32)
    time_scale = jnp.exp(jax.random.uniform(keys[3], (TIME,), jnp.float32, jnp.log(0.3), jnp.log(3.3)))
    point_scale = jnp.exp(jax.random.uniform(keys[4], (POINTS,), jnp.float32, jnp.log(0.3), jnp.log(3.3)))
    noise = jax.random.truncated_normal(keys[2], -4.0, 4.0, (TIME, POINTS), jnp.float32)
    coherent = jnp.zeros((TIME, POINTS), jnp.float32)
    for index in range(ranks):
        coherent = coherent + amps[:, index:index + 1] * shapes[index][None, :]
    field = coherent * (1.5 / 2.8284271) + noise
    return time_scale[:, None] * point_scale[None, :] * field


def steps_of(own_key, shape, cuts, smallest, high):
    def one(position, shards_of):
        steps = jax.random.uniform(jax.random.fold_in(jax.random.fold_in(own_key, 6), position), (shards_of,), jnp.float32, smallest / len(cuts), high / len(cuts))
        return jnp.repeat(jnp.exp(steps), shape[position] // shards_of).reshape((-1,) + (1,) * (len(shape) - position - 1))

    level = one(*cuts[0])
    for cut in cuts[1:]:
        level = level * one(*cut)
    return level


def setup_inputs(seed: int = 0) -> dict:
    arg_keys = jax.random.split(jax.random.key(seed), 3)
    snapshots = draw_snapshots(jax.random.fold_in(arg_keys[2], 71), 0)
    weights = jnp.clip(jnp.exp(math.log(4.0) - 2.7725887 * jax.random.uniform(arg_keys[1], (POINTS,), jnp.float32) ** steps_of(arg_keys[1], (POINTS,), ((0, 32),), -0.2, 0.2)), 0.25, 4.0)
    return {"snapshots": snapshots, "weights": weights}


HIGH = lax.Precision.HIGHEST

def dft_table(length, freqs):
    steps = jnp.arange(length, dtype=jnp.int32)
    orders = jnp.arange(freqs, dtype=jnp.int32)
    phase = (steps[:, None] * orders[None, :] % length).astype(jnp.float32)
    angle = 2.0 * math.pi * phase / length
    window = 0.5 - 0.5 * jnp.cos(2.0 * math.pi * steps.astype(jnp.float32) / length)
    norm = math.sqrt(3.0 * length / 8.0)
    real_part = window[:, None] * jnp.cos(angle) / norm
    imag_part = -window[:, None] * jnp.sin(angle) / norm
    return jnp.stack([real_part, imag_part], axis=2)

def rebuild(spectra, gram_real, gram_imag):
    nblocks = gram_real.shape[1]
    rows = jnp.arange(nblocks, dtype=jnp.float32)
    orders = jnp.arange(NMODE, dtype=jnp.float32)
    basis = jnp.cos(math.pi * (rows[:, None] + 0.5) * orders[None, :] / nblocks)
    trace = jnp.trace(gram_real, axis1=1, axis2=2) + 1e-06
    scale = (nblocks / trace)[:, None, None]
    first_real = scale * jnp.einsum('fab,bm->fam', gram_real, basis, precision=HIGH)
    first_imag = scale * jnp.einsum('fab,bm->fam', gram_imag, basis, precision=HIGH)
    second_real = scale * (jnp.einsum('fab,fbm->fam', gram_real, first_real, precision=HIGH) - jnp.einsum('fab,fbm->fam', gram_imag, first_imag, precision=HIGH))
    second_imag = scale * (jnp.einsum('fab,fbm->fam', gram_real, first_imag, precision=HIGH) + jnp.einsum('fab,fbm->fam', gram_imag, first_real, precision=HIGH))
    spec_real = spectra[:, 0]
    spec_imag = spectra[:, 1]
    mode_real = (jnp.einsum('fbx,fbm->fmx', spec_real, second_real, precision=HIGH) - jnp.einsum('fbx,fbm->fmx', spec_imag, second_imag, precision=HIGH)) / nblocks
    mode_imag = (jnp.einsum('fbx,fbm->fmx', spec_real, second_imag, precision=HIGH) + jnp.einsum('fbx,fbm->fmx', spec_imag, second_real, precision=HIGH)) / nblocks
    return jnp.stack([mode_real, mode_imag], axis=1)

def reference(snapshots, weights):
    table = dft_table(NFFT, NFREQ).reshape(NFFT, 2 * NFREQ)

    def one_block(index):
        piece = lax.dynamic_slice_in_dim(snapshots, index * STRIDE, NFFT, 0)
        return jnp.dot(table.T, piece, precision=HIGH).reshape(NFREQ, 2, POINTS)
    blocks = lax.map(one_block, jnp.arange(NB, dtype=jnp.int32))

    def one_freq(index):
        single = lax.dynamic_index_in_dim(blocks, index, 1, keepdims=False)
        spec_real = single[:, 0]
        spec_imag = single[:, 1]
        gram_real = (jnp.dot(spec_real, (spec_real * weights).T, precision=HIGH) + jnp.dot(spec_imag, (spec_imag * weights).T, precision=HIGH)) / POINTS
        gram_imag = (jnp.dot(spec_real, (spec_imag * weights).T, precision=HIGH) - jnp.dot(spec_imag, (spec_real * weights).T, precision=HIGH)) / POINTS
        spectra = jnp.transpose(single, (1, 0, 2))[None]
        built = rebuild(spectra, gram_real[None], gram_imag[None])[0]
        return (built, jnp.stack([gram_real, gram_imag], axis=0))
    modes, cross_spectra = lax.map(one_freq, jnp.arange(NFREQ, dtype=jnp.int32))
    return (modes, cross_spectra)
```

```python
import functools
import math

import jax
import jax.numpy as jnp
import ml_dtypes
import numpy as np
from jax import lax
from jax.experimental import pallas as pl
from jax.experimental.pallas import tpu as pltpu
from jax.sharding import PartitionSpec as P

NFFT = 256
STRIDE = 128
NFREQ = 64
NMODE = 4
NB = 31
TM = 8
OWN = NFREQ // TM
CHIPS = 16
LAG = 2
MESH = pl.DeviceIdType.MESH
F32 = jnp.float32
BF16 = jnp.bfloat16
HIGHEST = lax.Precision.HIGHEST
NN = (((1,), (0,)), ((), ()))
NT = (((1,), (1,)), ((), ()))


def row_plan():
    rows = []
    for d in range(TM):
        if d <= 3:
            rows.append((d, "close"))
        elif d == 4:
            rows.append((0, "open"))
        else:
            rows.append((d, "open"))
        rows.extend((d, j) for j in range(3))
    rows.extend((d, "open") for d in (1, 2, 3, 4))
    rows.extend((d, "close") for d in (7, 6, 5, 4))
    return rows


def tables(strides):
    steps = np.arange(NFFT)
    window = 0.5 - 0.5 * np.cos(2.0 * np.pi * steps / NFFT)
    angle = 2.0 * np.pi * ((steps[None, :] * np.arange(NFREQ)[:, None]) % NFFT) / NFFT
    norm = math.sqrt(3.0 * NFFT / 8.0)
    wave = np.stack([window * np.cos(angle) / norm, -window * np.sin(angle) / norm], axis=1)
    plan = row_plan()
    full = np.zeros((TM, OWN, 2 * len(plan), strides * STRIDE), np.float32)
    for me in range(TM):
        for place, (d, kind) in enumerate(plan):
            owner = (me + d) % TM
            part = wave[owner * OWN : (owner + 1) * OWN]
            row = full[me, :, 2 * place : 2 * place + 2]
            if kind == "close":
                row[:, :, :STRIDE] = part[:, :, STRIDE:]
            elif kind == "open":
                row[:, :, (strides - 1) * STRIDE :] = part[:, :, :STRIDE]
            else:
                row[:, :, kind * STRIDE : kind * STRIDE + NFFT] = part
    high = full.astype(ml_dtypes.bfloat16)
    low = (full - high.astype(np.float32)).astype(ml_dtypes.bfloat16)
    return np.concatenate([high, low], axis=2)


def block_order(me):
    order = []
    for slot in range(TM):
        source = me + slot
        if slot == 4:
            order.append(4 * me + 3)
        elif slot in (1, 2, 3):
            order.append(4 * source + 3)
        else:
            order.append(4 * source - 1)
        order.extend(4 * source + j for j in range(3))
    return [b % (NB + 1) for b in order]


PACK_V0, PACK_COL, PACK_ROW, PACK_C0, PACK_C1, PACK_END = 0, 8, 136, 168, 232, 296


def small_tables():
    pack = np.zeros((TM, PACK_END, 128), np.float32)
    b = np.arange(NB)
    m = np.arange(NMODE)
    basis = np.cos(np.pi * (b[:, None] + 0.5) * m[None, :] / NB)
    swap = np.zeros((64, 64), np.float32)
    for i in range(32):
        swap[2 * i + 1, 2 * i] = 1.0
        swap[2 * i, 2 * i + 1] = -1.0
    eye = np.eye(64, dtype=np.float32)
    for me in range(TM):
        for place, block in enumerate(block_order(me)):
            if block < NB:
                pack[me, PACK_V0 : PACK_V0 + 4, 2 * place] = basis[block]
                pack[me, PACK_V0 + 4 : PACK_V0 + 8, 2 * place + 1] = basis[block]
            pack[me, PACK_COL + 2 * place, block] = 1.0
            pack[me, PACK_COL + 2 * place + 1, 32 + block] = 1.0
            pack[me, PACK_ROW + block, place] = 1.0
        pack[me, PACK_C0 : PACK_C0 + 64, :64] = eye
        pack[me, PACK_C0 : PACK_C0 + 64, 64:] = -swap
        pack[me, PACK_C1 : PACK_C1 + 64, :64] = swap
        pack[me, PACK_C1 : PACK_C1 + 64, 64:] = eye
    return pack


def split(value):
    high = value.astype(BF16)
    return high, (value - high.astype(F32)).astype(BF16)


def dot(a, b, dims=NN, precision=None):
    return lax.dot_general(a, b, dims, precision=precision, preferred_element_type=F32)


def kernel(
    x_hbm, w_ref, table_hbm, pack_hbm, modes_ref, cross_ref,
    x, xh, xl, table, pack, made, halo_out, halo_in, got, ah, al, gram, core_out, core_in, chip_all,
    load_sem, table_sem, halo_ssem, halo_rsem, send_sem, recv_sem, core_ssem, core_rsem, chip_ssem, chip_rsem,
):
    points = x.shape[1]
    me = lax.axis_index("tm")
    space = lax.axis_index("space")
    core = lax.rem(space, 2)
    chip = space // 2
    cx = chip // 4
    cy = lax.rem(chip, 4)

    def along(d):
        return (lax.rem(me + d + TM, TM), space)

    others = [(i, j) for i in range(4) for j in range(4) if i or j]
    others.sort(key=lambda ij: -(min(ij[0], 4 - ij[0]) + min(ij[1], 4 - ij[1])))

    def chip_of(i, j):
        return lax.rem(cx + i, 4) * 4 + lax.rem(cy + j, 4)

    def across(i, j):
        return (me, chip_of(i, j) * 2 + core)

    mate = (me, chip * 2 + 1 - core)

    barrier = pltpu.get_barrier_semaphore()
    for d in range(1, TM):
        pl.semaphore_signal(barrier, inc=1, device_id=along(d), device_id_type=MESH)
    for i, j in others:
        pl.semaphore_signal(barrier, inc=1, device_id=across(i, j), device_id_type=MESH)
    pl.semaphore_signal(barrier, inc=1, device_id=mate, device_id_type=MESH)

    pieces = x.shape[0] // STRIDE

    def load_x(p):
        rows = pl.ds(p * STRIDE, STRIDE)
        return pltpu.make_async_copy(x_hbm.at[rows], x.at[rows], load_sem.at[p])

    def load_pack():
        return pltpu.make_async_copy(pack_hbm.at[me], pack, load_sem.at[pieces])

    def load_table(c):
        return pltpu.make_async_copy(table_hbm.at[me, c], table.at[c], table_sem.at[c])

    for p in range(pieces):
        load_x(p).start()
    load_table(0).start()
    load_pack().start()
    for c in range(1, OWN):
        load_table(c).start()
    for p in range(pieces):
        load_x(p).wait()
        rows = pl.ds(p * STRIDE, STRIDE)
        high, low = split(x[rows, :])
        xh[rows, :] = high
        xl[rows, :] = low
    load_pack().wait()

    def halo_copy(c, side):
        return pltpu.make_async_remote_copy(
            src_ref=halo_out.at[c, side], dst_ref=halo_in.at[c, side],
            send_sem=halo_ssem.at[c, side], recv_sem=halo_rsem.at[c, side],
            device_id=along(1 if side == 0 else -1), device_id_type=MESH,
        )

    def tile_copy(c, d):
        slot = (TM - d) % TM
        rows = pl.ds(2, 6) if d == 4 else pl.ds(0, 8)
        return pltpu.make_async_remote_copy(
            src_ref=made.at[c, d, rows], dst_ref=got.at[c, slot, rows],
            send_sem=send_sem.at[c, d], recv_sem=recv_sem.at[c, slot],
            device_id=along(d), device_id_type=MESH,
        )

    def core_copy(c):
        return pltpu.make_async_remote_copy(
            src_ref=core_out.at[c], dst_ref=core_in.at[c],
            send_sem=core_ssem.at[c], recv_sem=core_rsem.at[c],
            device_id=mate, device_id_type=MESH,
        )

    def chip_copy(c, n, i, j):
        return pltpu.make_async_remote_copy(
            src_ref=chip_all.at[c, chip], dst_ref=chip_all.at[c, chip],
            send_sem=chip_ssem.at[c, n], recv_sem=chip_rsem.at[c, chip],
            device_id=across(i, j), device_id_type=MESH,
        )

    def chip_arrival(c, n, i, j):
        source = chip_of(i, j)
        return pltpu.make_async_remote_copy(
            src_ref=chip_all.at[c, source], dst_ref=chip_all.at[c, source],
            send_sem=chip_ssem.at[c, n], recv_sem=chip_rsem.at[c, source],
            device_id=across(i, j), device_id_type=MESH,
        )

    def make(c):
        load_table(c).wait()
        for n in range(points // 256):
            columns = pl.ds(n * 256, 256)
            both = dot(table[c], xh[:, columns])
            value = both[:80] + both[80:] + dot(table[c, :80, :], xl[:, columns])
            for d in range(TM):
                made[c, d, :, columns] = value[8 * d : 8 * d + 8]
            halo_out[c, 0, :, columns] = value[64:72]
            halo_out[c, 1, :, columns] = value[72:80]

    def send_first(c):
        halo_copy(c, 0).start()
        halo_copy(c, 1).start()
        tile_copy(c, 4).start()

    def send_rest(c):
        halo_copy(c, 0).wait_recv()
        halo_copy(c, 1).wait_recv()
        first = me == 0
        last = me == TM - 1
        for d in range(4):
            total = made[c, d, 0:2, :] + halo_in[c, 0, 2 * d : 2 * d + 2, :]
            made[c, d, 0:2, :] = jnp.where(first, 0.0, total)
        for n, d in enumerate((4, 7, 6, 5)):
            total = made[c, d, 0:2, :] + halo_in[c, 1, 2 * n : 2 * n + 2, :]
            made[c, d, 0:2, :] = jnp.where(last, 0.0, total)
        for d in (5, 3, 6, 2, 7, 1):
            tile_copy(c, d).start()

    def correlate(c):
        for d in (4, 5, 3, 6, 2, 7, 1):
            tile_copy(c, d).wait_recv()
        own_rows = lax.broadcasted_iota(jnp.int32, (8, points), 0) < 2
        tiles = [made[c, 0]]
        for slot in range(1, TM):
            tile = got[c, slot]
            if slot == 4:
                tile = jnp.where(own_rows, made[c, 4], tile)
            tiles.append(tile)
        value = jnp.concatenate(tiles, axis=0)
        high, low = split(value)
        ah[c] = high
        al[c] = low
        whigh, wlow = split(value * w_ref[...])
        gram[...] = (
            dot(high, whigh, NT) + dot(high, wlow, NT) + dot(low, whigh, NT)
        )
        even = gram[pl.ds(0, 32, stride=2), :]
        odd = gram[pl.ds(1, 32, stride=2), :]
        core_out[c] = (
            dot(even, pack[PACK_C0 : PACK_C0 + 64, :], precision=HIGHEST)
            + dot(odd, pack[PACK_C1 : PACK_C1 + 64, :], precision=HIGHEST)
        )
        core_copy(c).start()

    def spread(c):
        core_copy(c).wait_recv()
        chip_all[c, chip] = core_out[c] + core_in[c]
        for n, (i, j) in enumerate(others):
            chip_copy(c, n, i, j).start()

    def finish(c):
        for n, (i, j) in enumerate(others):
            chip_arrival(c, n, i, j).wait_recv()
        parts = [chip_all[c, n] for n in range(CHIPS)]
        while len(parts) > 1:
            parts = [parts[n] + parts[n + 1] for n in range(0, len(parts), 2)]
        total = parts[0] / (points * 2 * CHIPS)
        rows = lax.broadcasted_iota(jnp.int32, total.shape, 0)
        lanes = lax.broadcasted_iota(jnp.int32, total.shape, 1)
        trace = jnp.sum(jnp.where(lanes == 2 * rows, total, 0.0)) + 1e-06
        scale = NB / trace
        wide = jnp.concatenate([total, pltpu.roll(total, 64, 1)], axis=0)[:, :64]
        one = scale * dot(pack[PACK_V0 : PACK_V0 + 8, :64], wide, NT, HIGHEST)
        two = scale * dot(one, wide, NN, HIGHEST)
        high, low = split(two)
        built = dot(high, ah[c]) + dot(high, al[c]) + dot(low, ah[c])
        modes_ref[c] = built / NB
        ordered = dot(total, pack[PACK_COL : PACK_COL + 128, :], precision=HIGHEST)
        ordered = dot(pack[PACK_ROW : PACK_ROW + 32, :32], ordered, precision=HIGHEST)
        cross_ref[c, 0] = ordered[:NB, :NB]
        cross_ref[c, 1] = pltpu.roll(ordered, 96, 1)[:NB, :NB]

    make(0)
    pl.semaphore_wait(barrier, (TM - 1) + len(others) + 1)
    send_first(0)

    def step(s, carry):
        @pl.when(s < OWN)
        def _():
            make(s)
            send_first(s)

        @pl.when(s <= OWN)
        def _():
            send_rest(s - 1)

        @pl.when((s >= LAG) & (s < OWN + LAG))
        def _():
            correlate(s - LAG)
            spread(s - LAG)

        @pl.when(s >= LAG + 1)
        def _():
            finish(s - LAG - 1)

        return carry

    lax.fori_loop(1, OWN + LAG + 1, step, 0)

    def drain(c, carry):
        halo_copy(c, 0).wait_send()
        halo_copy(c, 1).wait_send()
        for d in range(1, TM):
            tile_copy(c, d).wait_send()
        core_copy(c).wait_send()
        for n, (i, j) in enumerate(others):
            chip_copy(c, n, i, j).wait_send()
        return carry

    lax.fori_loop(0, OWN, drain, 0)


def local(snapshots, weights):
    steps, points = snapshots.shape
    table = jnp.asarray(tables(steps // STRIDE))
    pack = jnp.asarray(small_tables())
    rows = table.shape[2]
    any_space = pl.BlockSpec(memory_space=pl.ANY)
    vmem = pl.BlockSpec(memory_space=pltpu.VMEM)
    dma = pltpu.SemaphoreType.DMA
    modes, cross = pl.pallas_call(
        kernel,
        out_shape=(
            jax.ShapeDtypeStruct((OWN, 2 * NMODE, points), F32),
            jax.ShapeDtypeStruct((OWN, 2, NB, NB), F32),
        ),
        in_specs=[any_space, vmem, any_space, any_space],
        out_specs=(vmem, vmem),
        scratch_shapes=[
            pltpu.VMEM((steps, points), F32),
            pltpu.VMEM((steps, points), BF16),
            pltpu.VMEM((steps, points), BF16),
            pltpu.VMEM((OWN, rows, steps), BF16),
            pltpu.VMEM((PACK_END, 128), F32),
            pltpu.VMEM((OWN, TM, 8, points), F32),
            pltpu.VMEM((OWN, 2, 8, points), F32),
            pltpu.VMEM((OWN, 2, 8, points), F32),
            pltpu.VMEM((OWN, TM, 8, points), F32),
            pltpu.VMEM((OWN, 64, points), BF16),
            pltpu.VMEM((OWN, 64, points), BF16),
            pltpu.VMEM((64, 64), F32),
            pltpu.VMEM((OWN, 32, 128), F32),
            pltpu.VMEM((OWN, 32, 128), F32),
            pltpu.VMEM((OWN, CHIPS, 32, 128), F32),
            dma((steps // STRIDE + 1,)),
            dma((OWN,)),
            dma((OWN, 2)),
            dma((OWN, 2)),
            dma((OWN, TM)),
            dma((OWN, TM)),
            dma((OWN,)),
            dma((OWN,)),
            dma((OWN, CHIPS)),
            dma((OWN, CHIPS)),
        ],
        compiler_params=pltpu.CompilerParams(
            collective_id=0, has_side_effects=True, vmem_limit_bytes=48 << 20
        ),
        cost_estimate=pl.CostEstimate(flops=4 << 30, bytes_accessed=8 << 20, transcendentals=0),
        name="spod",
    )(snapshots, weights.reshape(1, points), table, pack)
    return modes.reshape(OWN, 2, NMODE, points), cross


def solution(mesh):
    return jax.shard_map(
        local,
        mesh=mesh,
        in_specs=(P("tm", "space"), P("space")),
        out_specs=(P("tm", None, None, "space"), P("tm", None, None, None)),
        check_vma=False,
    )
```

```python
import functools
import math

import jax
import jax.numpy as jnp
import ml_dtypes
import numpy as np
from jax import lax
from jax.experimental import pallas as pl
from jax.experimental.pallas import tpu as pltpu
from jax.sharding import PartitionSpec as P

NFFT = 256
STRIDE = 128
NFREQ = 64
NMODE = 4
NB = 31
TM = 8
OWN = NFREQ // TM
CHIPS = 16
LAG = 2
WAIT = 2
MESH = pl.DeviceIdType.MESH
F32 = jnp.float32
BF16 = jnp.bfloat16
HIGHEST = lax.Precision.HIGHEST
NN = (((1,), (0,)), ((), ()))
NT = (((1,), (1,)), ((), ()))


def row_plan():
    rows = []
    for d in range(TM):
        if d <= 3:
            rows.append((d, "close"))
        elif d == 4:
            rows.append((0, "open"))
        else:
            rows.append((d, "open"))
        rows.extend((d, j) for j in range(3))
    rows.extend((d, "open") for d in (1, 2, 3, 4))
    rows.extend((d, "close") for d in (7, 6, 5, 4))
    return rows


def tables(strides):
    steps = np.arange(NFFT)
    window = 0.5 - 0.5 * np.cos(2.0 * np.pi * steps / NFFT)
    angle = 2.0 * np.pi * ((steps[None, :] * np.arange(NFREQ)[:, None]) % NFFT) / NFFT
    norm = math.sqrt(3.0 * NFFT / 8.0)
    wave = np.stack([window * np.cos(angle) / norm, -window * np.sin(angle) / norm], axis=1)
    plan = row_plan()
    full = np.zeros((TM, OWN, 2 * len(plan), strides * STRIDE), np.float32)
    for me in range(TM):
        for place, (d, kind) in enumerate(plan):
            owner = (me + d) % TM
            part = wave[owner * OWN : (owner + 1) * OWN]
            row = full[me, :, 2 * place : 2 * place + 2]
            if kind == "close":
                row[:, :, :STRIDE] = part[:, :, STRIDE:]
            elif kind == "open":
                row[:, :, (strides - 1) * STRIDE :] = part[:, :, :STRIDE]
            else:
                row[:, :, kind * STRIDE : kind * STRIDE + NFFT] = part
    high = full.astype(ml_dtypes.bfloat16)
    low = (full - high.astype(np.float32)).astype(ml_dtypes.bfloat16)
    return np.concatenate([high, low], axis=2)


def block_order(me):
    order = []
    for slot in range(TM):
        source = me + slot
        if slot == 4:
            order.append(4 * me + 3)
        elif slot in (1, 2, 3):
            order.append(4 * source + 3)
        else:
            order.append(4 * source - 1)
        order.extend(4 * source + j for j in range(3))
    return [b % (NB + 1) for b in order]


PACK_V0, PACK_COL, PACK_ROW, PACK_SWAP, PACK_END = 0, 8, 72, 104, 168


def small_tables():
    pack = np.zeros((TM, PACK_END, 128), np.float32)
    b = np.arange(NB)
    m = np.arange(NMODE)
    basis = np.cos(np.pi * (b[:, None] + 0.5) * m[None, :] / NB)
    swap = np.zeros((64, 64), np.float32)
    for i in range(32):
        swap[2 * i + 1, 2 * i] = 1.0
        swap[2 * i, 2 * i + 1] = -1.0
    for me in range(TM):
        for place, block in enumerate(block_order(me)):
            if block < NB:
                pack[me, PACK_V0 : PACK_V0 + 4, 2 * place] = basis[block]
                pack[me, PACK_V0 + 4 : PACK_V0 + 8, 2 * place + 1] = basis[block]
            pack[me, PACK_COL + 2 * place, block] = 1.0
            pack[me, PACK_COL + 2 * place + 1, 32 + block] = 1.0
            pack[me, PACK_ROW + block, place] = 1.0
        pack[me, PACK_SWAP : PACK_SWAP + 64, :64] = swap
    return pack


def split(value):
    high = value.astype(BF16)
    return high, (value - high.astype(F32)).astype(BF16)


def dot(a, b, dims=NN, precision=None):
    return lax.dot_general(a, b, dims, precision=precision, preferred_element_type=F32)


def kernel(
    x_hbm, w_hbm, table_hbm, pack_hbm, modes_ref, cross_ref,
    x, w_ref, xh, xl, table, pack, made, halo_out, halo_in, got, ah, al, gram, core_out, core_in, chip_all,
    load_sem, table_sem, send_sem, halo_rsem, tile_rsem, far_rsem, core_rsem, chip_rsem,
):
    points = x.shape[1]
    me = lax.axis_index("tm")
    space = lax.axis_index("space")
    core = lax.rem(space, 2)
    chip = space // 2
    cx = chip // 4
    cy = lax.rem(chip, 4)

    def along(d):
        return (lax.rem(me + d + TM, TM), space)

    others = [(i, j) for i in range(4) for j in range(4) if i or j]
    others.sort(key=lambda ij: -(min(ij[0], 4 - ij[0]) + min(ij[1], 4 - ij[1])))

    def chip_of(i, j):
        return lax.rem(cx + i, 4) * 4 + lax.rem(cy + j, 4)

    def across(i, j):
        return (me, chip_of(i, j) * 2 + core)

    mate = (me, chip * 2 + 1 - core)

    pieces = points // 256

    def load_x(p):
        columns = pl.ds(p * 256, 256)
        return pltpu.make_async_copy(x_hbm.at[:, columns], x.at[:, columns], load_sem.at[p])

    def load_pack():
        return pltpu.make_async_copy(pack_hbm.at[me], pack, load_sem.at[pieces])

    def load_w():
        return pltpu.make_async_copy(w_hbm, w_ref, load_sem.at[pieces + 1])

    def load_table():
        return pltpu.make_async_copy(table_hbm.at[me, 0], table.at[0], table_sem.at[0])

    def load_tables():
        rest = pl.ds(1, OWN - 1)
        return pltpu.make_async_copy(table_hbm.at[me, rest], table.at[rest], table_sem.at[1])

    load_table().start()
    for p in range(pieces):
        load_x(p).start()
    load_pack().start()
    load_w().start()
    load_tables().start()
    barrier = pltpu.get_barrier_semaphore()
    for d in range(1, TM):
        pl.semaphore_signal(barrier, inc=1, device_id=along(d), device_id_type=MESH)
    for i, j in others:
        pl.semaphore_signal(barrier, inc=1, device_id=across(i, j), device_id_type=MESH)
    pl.semaphore_signal(barrier, inc=1, device_id=mate, device_id_type=MESH)


    def halo_copy(c, side):
        return pltpu.make_async_remote_copy(
            src_ref=halo_out.at[c, side], dst_ref=halo_in.at[c, side],
            send_sem=send_sem.at[0], recv_sem=halo_rsem.at[c],
            device_id=along(1 if side == 0 else -1), device_id_type=MESH,
        )

    def tile_copy(c, d):
        slot = (TM - d) % TM
        return pltpu.make_async_remote_copy(
            src_ref=made.at[c, d], dst_ref=got.at[c, slot],
            send_sem=send_sem.at[1], recv_sem=tile_rsem.at[c],
            device_id=along(d), device_id_type=MESH,
        )

    def far_copy(c):
        rows = pl.ds(2, 6)
        return pltpu.make_async_remote_copy(
            src_ref=made.at[c, 4, rows], dst_ref=got.at[c, 4, rows],
            send_sem=send_sem.at[2], recv_sem=far_rsem.at[c],
            device_id=along(4), device_id_type=MESH,
        )

    def core_copy(c):
        return pltpu.make_async_remote_copy(
            src_ref=core_out.at[c], dst_ref=core_in.at[c],
            send_sem=send_sem.at[3], recv_sem=core_rsem.at[c],
            device_id=mate, device_id_type=MESH,
        )

    def chip_copy(c, i, j):
        return pltpu.make_async_remote_copy(
            src_ref=chip_all.at[c, chip], dst_ref=chip_all.at[c, chip],
            send_sem=send_sem.at[4], recv_sem=chip_rsem.at[c],
            device_id=across(i, j), device_id_type=MESH,
        )

    def whole(ref, kind, sem):
        return pltpu.make_async_remote_copy(
            src_ref=ref, dst_ref=ref, send_sem=send_sem.at[kind], recv_sem=sem,
            device_id=mate, device_id_type=MESH,
        )

    def make(c, opening=False):
        if opening:
            load_table().wait()
        for n in range(pieces):
            columns = pl.ds(n * 256, 256)
            if opening:
                load_x(n).wait()
                high, low = split(x[:, columns])
                xh[:, columns] = high
                xl[:, columns] = low
            both = dot(table[c], xh[:, columns])
            value = both[:80] + both[80:] + dot(table[c, :80, :], xl[:, columns])
            for d in range(TM):
                made[c, d, :, columns] = value[8 * d : 8 * d + 8]
            halo_out[c, 0, :, columns] = value[64:72]
            halo_out[c, 1, :, columns] = value[72:80]

    def send_first(c):
        halo_copy(c, 0).start()
        halo_copy(c, 1).start()
        far_copy(c).start()

    def send_rest(c):
        whole(halo_in.at[c], 0, halo_rsem.at[c]).wait_recv()
        first = me == 0
        last = me == TM - 1
        for d in range(4):
            total = made[c, d, 0:2, :] + halo_in[c, 0, 2 * d : 2 * d + 2, :]
            made[c, d, 0:2, :] = jnp.where(first, 0.0, total)
        for n, d in enumerate((4, 7, 6, 5)):
            total = made[c, d, 0:2, :] + halo_in[c, 1, 2 * n : 2 * n + 2, :]
            made[c, d, 0:2, :] = jnp.where(last, 0.0, total)
        for d in (5, 3, 6, 2, 7, 1):
            tile_copy(c, d).start()

    def correlate(c):
        far_copy(c).wait_recv()
        whole(got.at[c, pl.ds(0, 6)], 1, tile_rsem.at[c]).wait_recv()
        own_rows = lax.broadcasted_iota(jnp.int32, (8, points), 0) < 2
        tiles = [made[c, 0]]
        for slot in range(1, TM):
            tile = got[c, slot]
            if slot == 4:
                tile = jnp.where(own_rows, made[c, 4], tile)
            tiles.append(tile)
        value = jnp.concatenate(tiles, axis=0)
        high, low = split(value)
        ah[c] = high
        al[c] = low
        whigh, wlow = split(value * w_ref[...])
        gram[...] = (
            dot(high, whigh, NT) + dot(high, wlow, NT) + dot(low, whigh, NT)
        )
        even = gram[pl.ds(0, 32, stride=2), :]
        odd = gram[pl.ds(1, 32, stride=2), :]
        kept = even + dot(odd, pack[PACK_SWAP : PACK_SWAP + 64, :64], precision=HIGHEST)
        core_out[c] = jnp.concatenate([kept[:16], kept[16:]], axis=1)
        core_copy(c).start()

    def spread(c):
        core_copy(c).wait_recv()
        chip_all[c, chip] = core_out[c] + core_in[c]
        for i, j in others:
            chip_copy(c, i, j).start()

    def finish(c):
        whole(chip_all.at[c, pl.ds(0, CHIPS - 1)], 4, chip_rsem.at[c]).wait_recv()
        parts = [chip_all[c, n] for n in range(CHIPS)]
        while len(parts) > 1:
            parts = [parts[n] + parts[n + 1] for n in range(0, len(parts), 2)]
        total = parts[0] / (points * 2 * CHIPS)
        total = jnp.concatenate([total, pltpu.roll(total, 64, 1)], axis=0)
        rows = lax.broadcasted_iota(jnp.int32, total.shape, 0)
        lanes = lax.broadcasted_iota(jnp.int32, total.shape, 1)
        trace = jnp.sum(jnp.where(lanes == 2 * rows, total, 0.0)) + 1e-06
        scale = NB / trace
        odd = jnp.where(lanes % 2 == 0, -pltpu.roll(total, 127, 1), pltpu.roll(total, 1, 1))
        wide = jnp.concatenate([total, odd], axis=0)[:, :64]
        one = scale * dot(pack[PACK_V0 : PACK_V0 + 8, :64], wide, NT, HIGHEST)
        two = scale * dot(one, wide, NN, HIGHEST)
        high, low = split(two)
        built = dot(high, ah[c]) + dot(high, al[c]) + dot(low, ah[c])
        built = built / NB
        modes_ref[c, 0] = built[:NMODE]
        modes_ref[c, 1] = built[NMODE:]
        ordered = dot(total[:, :64], pack[PACK_COL : PACK_COL + 64, :], precision=HIGHEST)
        ordered = dot(pack[PACK_ROW : PACK_ROW + 32, :32], ordered, precision=HIGHEST)
        cross_ref[c, 0] = ordered[:NB, :NB]
        cross_ref[c, 1] = pltpu.roll(ordered, 96, 1)[:NB, :NB]

    make(0, opening=True)
    pl.semaphore_wait(barrier, (TM - 1) + len(others) + 1)
    send_first(0)
    load_pack().wait()
    load_w().wait()
    load_tables().wait()

    def step(s, carry):
        @pl.when(s < OWN)
        def _():
            make(s)
            send_first(s)

        @pl.when(s <= OWN)
        def _():
            send_rest(s - 1)

        @pl.when((s >= LAG) & (s < OWN + LAG))
        def _():
            correlate(s - LAG)
            spread(s - LAG)

        @pl.when(s >= LAG + WAIT)
        def _():
            finish(s - LAG - WAIT)

        return carry

    lax.fori_loop(1, OWN + LAG + WAIT, step, 0)

    whole(halo_out, 0, core_rsem.at[0]).wait_send()
    whole(made.at[:, pl.ds(0, 6)], 1, core_rsem.at[0]).wait_send()
    whole(made.at[:, 4, pl.ds(2, 6)], 2, core_rsem.at[0]).wait_send()
    whole(core_out, 3, core_rsem.at[0]).wait_send()
    whole(chip_all.at[:, pl.ds(0, CHIPS - 1)], 4, core_rsem.at[0]).wait_send()


def local(snapshots, weights):
    steps, points = snapshots.shape
    table = jnp.asarray(tables(steps // STRIDE))
    pack = jnp.asarray(small_tables())
    rows = table.shape[2]
    any_space = pl.BlockSpec(memory_space=pl.ANY)
    vmem = pl.BlockSpec(memory_space=pltpu.VMEM)
    dma = pltpu.SemaphoreType.DMA
    modes, cross = pl.pallas_call(
        kernel,
        out_shape=(
            jax.ShapeDtypeStruct((OWN, 2, NMODE, points), F32),
            jax.ShapeDtypeStruct((OWN, 2, NB, NB), F32),
        ),
        in_specs=[any_space, any_space, any_space, any_space],
        out_specs=(vmem, vmem),
        scratch_shapes=[
            pltpu.VMEM((steps, points), F32),
            pltpu.VMEM((1, points), F32),
            pltpu.VMEM((steps, points), BF16),
            pltpu.VMEM((steps, points), BF16),
            pltpu.VMEM((OWN, rows, steps), BF16),
            pltpu.VMEM((PACK_END, 128), F32),
            pltpu.VMEM((OWN, TM, 8, points), F32),
            pltpu.VMEM((OWN, 2, 8, points), F32),
            pltpu.VMEM((OWN, 2, 8, points), F32),
            pltpu.VMEM((OWN, TM, 8, points), F32),
            pltpu.VMEM((OWN, 64, points), BF16),
            pltpu.VMEM((OWN, 64, points), BF16),
            pltpu.VMEM((64, 64), F32),
            pltpu.VMEM((OWN, 16, 128), F32),
            pltpu.VMEM((OWN, 16, 128), F32),
            pltpu.VMEM((OWN, CHIPS, 16, 128), F32),
            dma((points // 256 + 2,)),
            dma((2,)),
            dma((5,)),
            dma((OWN,)),
            dma((OWN,)),
            dma((OWN,)),
            dma((OWN,)),
            dma((OWN,)),
        ],
        compiler_params=pltpu.CompilerParams(
            collective_id=0, has_side_effects=True, vmem_limit_bytes=52 << 20
        ),
        cost_estimate=pl.CostEstimate(flops=4 << 30, bytes_accessed=8 << 20, transcendentals=0),
        name="spod",
    )(snapshots, weights.reshape(1, points), table, pack)
    return modes, cross


def solution(mesh):
    return jax.shard_map(
        local,
        mesh=mesh,
        in_specs=(P("tm", "space"), P("space")),
        out_specs=(P("tm", None, None, "space"), P("tm", None, None, None)),
        check_vma=False,
    )
```

```python
import functools
import math

import jax
import jax.numpy as jnp
import ml_dtypes
import numpy as np
from jax import lax
from jax.experimental import pallas as pl
from jax.experimental.pallas import tpu as pltpu
from jax.sharding import PartitionSpec as P

NFFT = 256
STRIDE = 128
NFREQ = 64
NMODE = 4
NB = 31
TM = 8
OWN = NFREQ // TM
CHIPS = 16
LAG = 2
WAIT = 2
ORDER = (0, 1, 2, 3, 7, 6, 5, 4)
ORDERED = 7
MESH = pl.DeviceIdType.MESH
F32 = jnp.float32
BF16 = jnp.bfloat16
HIGHEST = lax.Precision.HIGHEST
NN = (((1,), (0,)), ((), ()))
NT = (((1,), (1,)), ((), ()))


def row_plan():
    rows = []
    for d in range(TM):
        if d <= 3:
            rows.append((d, "close"))
        elif d == 4:
            rows.append((0, "open"))
        else:
            rows.append((d, "open"))
        rows.extend((d, j) for j in range(3))
    rows.extend((d, "open") for d in (1, 2, 3, 4))
    rows.extend((d, "close") for d in (7, 6, 5, 4))
    return rows


def tables(strides):
    steps = np.arange(NFFT)
    window = 0.5 - 0.5 * np.cos(2.0 * np.pi * steps / NFFT)
    angle = 2.0 * np.pi * ((steps[None, :] * np.arange(NFREQ)[:, None]) % NFFT) / NFFT
    norm = math.sqrt(3.0 * NFFT / 8.0)
    wave = np.stack([window * np.cos(angle) / norm, -window * np.sin(angle) / norm], axis=1)
    plan = row_plan()
    full = np.zeros((TM, OWN, 2 * len(plan), strides * STRIDE), np.float32)
    for me in range(TM):
        for place, (d, kind) in enumerate(plan):
            owner = (me + d) % TM
            part = wave[owner * OWN : (owner + 1) * OWN]
            row = full[me, :, 2 * place : 2 * place + 2]
            if kind == "close":
                row[:, :, :STRIDE] = part[:, :, STRIDE:]
            elif kind == "open":
                row[:, :, (strides - 1) * STRIDE :] = part[:, :, :STRIDE]
            else:
                row[:, :, kind * STRIDE : kind * STRIDE + NFFT] = part
    high = full.astype(ml_dtypes.bfloat16)
    low = (full - high.astype(np.float32)).astype(ml_dtypes.bfloat16)
    return np.concatenate([high, low], axis=2)


def block_order(me):
    order = []
    for slot in range(TM):
        source = me + slot
        if slot == 4:
            order.append(4 * me + 3)
        elif slot in (1, 2, 3):
            order.append(4 * source + 3)
        else:
            order.append(4 * source - 1)
        order.extend(4 * source + j for j in range(3))
    return [b % (NB + 1) for b in order]


PACK_V0, PACK_COL, PACK_ROW, PACK_SWAP, PACK_END = 0, 8, 72, 104, 168
PACK_WIDE = 1024


def small_tables():
    pack = np.zeros((TM, PACK_END, PACK_WIDE), np.float32)
    b = np.arange(NB)
    m = np.arange(NMODE)
    basis = np.cos(np.pi * (b[:, None] + 0.5) * m[None, :] / NB)
    swap = np.zeros((64, 64), np.float32)
    for i in range(32):
        swap[2 * i + 1, 2 * i] = 1.0
        swap[2 * i, 2 * i + 1] = -1.0
    for me in range(TM):
        for place, block in enumerate(block_order(me)):
            if block < NB:
                pack[me, PACK_V0 : PACK_V0 + 4, 2 * place] = basis[block]
                pack[me, PACK_V0 + 4 : PACK_V0 + 8, 2 * place + 1] = basis[block]
            pack[me, PACK_COL + 2 * place, block] = 1.0
            pack[me, PACK_COL + 2 * place + 1, 32 + block] = 1.0
            pack[me, PACK_ROW + block, place] = 1.0
        pack[me, PACK_SWAP : PACK_SWAP + 64, :64] = swap
    return pack


def split(value):
    high = value.astype(BF16)
    return high, (value - high.astype(F32)).astype(BF16)


def dot(a, b, dims=NN, precision=None):
    return lax.dot_general(a, b, dims, precision=precision, preferred_element_type=F32)


def kernel(
    x_hbm, w_hbm, table_hbm, pack_hbm, modes_ref, cross_ref,
    x, w_ref, xh, xl, table, pack, made, halo_out, halo_in, got, ah, al, gram, core_out, core_in, chip_all,
    load_sem, table_sem, send_sem, halo_rsem, tile_rsem, far_rsem, core_rsem, chip_rsem,
):
    points = x.shape[1]
    me = lax.axis_index("tm")
    space = lax.axis_index("space")
    core = lax.rem(space, 2)
    chip = space // 2
    cx = chip // 4
    cy = lax.rem(chip, 4)

    def along(d):
        return (lax.rem(me + d + TM, TM), space)

    others = [(i, j) for i in range(4) for j in range(4) if i or j]
    others.sort(key=lambda ij: -(min(ij[0], 4 - ij[0]) + min(ij[1], 4 - ij[1])))

    def chip_of(i, j):
        return lax.rem(cx + i, 4) * 4 + lax.rem(cy + j, 4)

    def across(i, j):
        return (me, chip_of(i, j) * 2 + core)

    mate = (me, chip * 2 + 1 - core)

    pieces = points // 256

    def load_x(p):
        columns = pl.ds(p * 256, 256)
        return pltpu.make_async_copy(x_hbm.at[:, columns], x.at[:, columns], load_sem.at[p])

    def load_pack():
        return pltpu.make_async_copy(
            pack_hbm.at[me, :, pl.ds(0, 128)], pack, load_sem.at[pieces]
        )

    def load_w():
        return pltpu.make_async_copy(w_hbm, w_ref, load_sem.at[pieces + 1])

    def load_table():
        return pltpu.make_async_copy(table_hbm.at[me, 0], table.at[0], table_sem.at[0])

    def load_tables():
        rest = pl.ds(1, OWN - 1)
        return pltpu.make_async_copy(table_hbm.at[me, rest], table.at[rest], table_sem.at[1])

    load_table().start()
    for p in range(pieces):
        load_x(p).start()
    load_pack().start()
    load_w().start()
    load_tables().start()
    barrier = pltpu.get_barrier_semaphore()
    for d in range(1, TM):
        pl.semaphore_signal(barrier, inc=1, device_id=along(d), device_id_type=MESH)
    for i, j in others:
        pl.semaphore_signal(barrier, inc=1, device_id=across(i, j), device_id_type=MESH)
    pl.semaphore_signal(barrier, inc=1, device_id=mate, device_id_type=MESH)


    def halo_copy(c, side):
        return pltpu.make_async_remote_copy(
            src_ref=halo_out.at[c, side], dst_ref=halo_in.at[c, side],
            send_sem=send_sem.at[0], recv_sem=halo_rsem.at[c],
            device_id=along(1 if side == 0 else -1), device_id_type=MESH,
        )

    def tile_copy(c, d):
        slot = lax.rem(TM - d, TM)
        return pltpu.make_async_remote_copy(
            src_ref=made.at[c, d], dst_ref=got.at[c, slot],
            send_sem=send_sem.at[1], recv_sem=tile_rsem.at[c],
            device_id=along(d), device_id_type=MESH,
        )

    def far_copy(c):
        rows = pl.ds(2, 6)
        return pltpu.make_async_remote_copy(
            src_ref=made.at[c, 4, rows], dst_ref=got.at[c, 4, rows],
            send_sem=send_sem.at[2], recv_sem=far_rsem.at[c],
            device_id=along(4), device_id_type=MESH,
        )

    def core_copy(c):
        return pltpu.make_async_remote_copy(
            src_ref=core_out.at[c], dst_ref=core_in.at[c],
            send_sem=send_sem.at[3], recv_sem=core_rsem.at[c],
            device_id=mate, device_id_type=MESH,
        )

    def chip_copy(c, i, j):
        return pltpu.make_async_remote_copy(
            src_ref=chip_all.at[c, chip], dst_ref=chip_all.at[c, chip],
            send_sem=send_sem.at[4], recv_sem=chip_rsem.at[c],
            device_id=across(i, j), device_id_type=MESH,
        )

    def whole(ref, kind, sem):
        return pltpu.make_async_remote_copy(
            src_ref=ref, dst_ref=ref, send_sem=send_sem.at[kind], recv_sem=sem,
            device_id=mate, device_id_type=MESH,
        )

    def make(c, opening=False):
        if opening:
            load_table().wait()
        for n in range(pieces):
            columns = pl.ds(n * 256, 256)
            if opening:
                load_x(n).wait()
                high, low = split(x[:, columns])
                xh[:, columns] = high
                xl[:, columns] = low
            both = dot(table[c], xh[:, columns])
            value = both[:80] + both[80:] + dot(table[c, :80, :], xl[:, columns])
            for d in range(TM):
                made[c, d, :, columns] = value[8 * d : 8 * d + 8]
            halo_out[c, 0, :, columns] = value[64:72]
            halo_out[c, 1, :, columns] = value[72:80]

    def send_first(c):
        halo_copy(c, 0).start()
        halo_copy(c, 1).start()

        @pl.when(c < ORDERED)
        def _():
            far_copy(c).start()

    def send_rest(c):
        whole(halo_in.at[c], 0, halo_rsem.at[c]).wait_recv()
        first = me == 0
        last = me == TM - 1
        for d in range(4):
            total = made[c, d, 0:2, :] + halo_in[c, 0, 2 * d : 2 * d + 2, :]
            made[c, d, 0:2, :] = jnp.where(first, 0.0, total)
        for n, d in enumerate((4, 7, 6, 5)):
            total = made[c, d, 0:2, :] + halo_in[c, 1, 2 * n : 2 * n + 2, :]
            made[c, d, 0:2, :] = jnp.where(last, 0.0, total)
        @pl.when(c < ORDERED)
        def _():
            for d in (5, 3, 6, 2, 7, 1):
                tile_copy(c, d).start()

        @pl.when(c >= ORDERED)
        def _():
            for owner in ORDER:
                d = lax.rem(owner - me + TM, TM)

                @pl.when((d != 0) & (d != 4))
                def _():
                    tile_copy(c, d).start()

                @pl.when(d == 4)
                def _():
                    far_copy(c).start()

    def correlate(c):
        far_copy(c).wait_recv()
        whole(got.at[c, pl.ds(0, 6)], 1, tile_rsem.at[c]).wait_recv()
        own_rows = lax.broadcasted_iota(jnp.int32, (8, points), 0) < 2
        tiles = [made[c, 0]]
        for slot in range(1, TM):
            tile = got[c, slot]
            if slot == 4:
                tile = jnp.where(own_rows, made[c, 4], tile)
            tiles.append(tile)
        value = jnp.concatenate(tiles, axis=0)
        high, low = split(value)
        ah[c] = high
        al[c] = low
        whigh, wlow = split(value * w_ref[...])
        gram[...] = (
            dot(high, whigh, NT) + dot(high, wlow, NT) + dot(low, whigh, NT)
        )
        even = gram[pl.ds(0, 32, stride=2), :]
        odd = gram[pl.ds(1, 32, stride=2), :]
        kept = even + dot(odd, pack[PACK_SWAP : PACK_SWAP + 64, :64], precision=HIGHEST)
        core_out[c] = jnp.concatenate([kept[:16], kept[16:]], axis=1)
        core_copy(c).start()

    def spread(c):
        core_copy(c).wait_recv()
        chip_all[c, chip] = core_out[c] + core_in[c]
        for i, j in others:
            chip_copy(c, i, j).start()

    def finish(c):
        whole(chip_all.at[c, pl.ds(0, CHIPS - 1)], 4, chip_rsem.at[c]).wait_recv()
        parts = [chip_all[c, n] for n in range(CHIPS)]
        while len(parts) > 1:
            parts = [parts[n] + parts[n + 1] for n in range(0, len(parts), 2)]
        total = parts[0] / (points * 2 * CHIPS)
        total = jnp.concatenate([total, pltpu.roll(total, 64, 1)], axis=0)
        rows = lax.broadcasted_iota(jnp.int32, total.shape, 0)
        lanes = lax.broadcasted_iota(jnp.int32, total.shape, 1)
        trace = jnp.sum(jnp.where(lanes == 2 * rows, total, 0.0)) + 1e-06
        scale = NB / trace
        odd = jnp.where(lanes % 2 == 0, -pltpu.roll(total, 127, 1), pltpu.roll(total, 1, 1))
        wide = jnp.concatenate([total, odd], axis=0)[:, :64]
        one = scale * dot(pack[PACK_V0 : PACK_V0 + 8, :64], wide, NT, HIGHEST)
        two = scale * dot(one, wide, NN, HIGHEST)
        high, low = split(two)
        built = dot(high, ah[c]) + dot(high, al[c]) + dot(low, ah[c])
        built = built / NB
        modes_ref[c, 0] = built[:NMODE]
        modes_ref[c, 1] = built[NMODE:]
        ordered = dot(total[:, :64], pack[PACK_COL : PACK_COL + 64, :], precision=HIGHEST)
        ordered = dot(pack[PACK_ROW : PACK_ROW + 32, :32], ordered, precision=HIGHEST)
        cross_ref[c, 0] = ordered[:NB, :NB]
        cross_ref[c, 1] = pltpu.roll(ordered, 96, 1)[:NB, :NB]

    make(0, opening=True)
    pl.semaphore_wait(barrier, (TM - 1) + len(others) + 1)
    send_first(0)
    load_pack().wait()
    load_w().wait()
    load_tables().wait()

    def step(s, carry):
        @pl.when(s < OWN)
        def _():
            make(s)
            send_first(s)

        @pl.when(s <= OWN)
        def _():
            send_rest(s - 1)

        @pl.when((s >= LAG) & (s < OWN + LAG))
        def _():
            correlate(s - LAG)
            spread(s - LAG)

        @pl.when(s >= LAG + WAIT)
        def _():
            finish(s - LAG - WAIT)

        return carry

    lax.fori_loop(1, OWN + LAG + WAIT, step, 0)

    whole(halo_out, 0, core_rsem.at[0]).wait_send()
    whole(made.at[:, pl.ds(0, 6)], 1, core_rsem.at[0]).wait_send()
    whole(made.at[:, 4, pl.ds(2, 6)], 2, core_rsem.at[0]).wait_send()
    whole(core_out, 3, core_rsem.at[0]).wait_send()
    whole(chip_all.at[:, pl.ds(0, CHIPS - 1)], 4, core_rsem.at[0]).wait_send()


def local(snapshots, weights):
    steps, points = snapshots.shape
    table = jnp.asarray(tables(steps // STRIDE))
    pack = jnp.asarray(small_tables())
    rows = table.shape[2]
    any_space = pl.BlockSpec(memory_space=pl.ANY)
    vmem = pl.BlockSpec(memory_space=pltpu.VMEM)
    dma = pltpu.SemaphoreType.DMA
    modes, cross = pl.pallas_call(
        kernel,
        out_shape=(
            jax.ShapeDtypeStruct((OWN, 2, NMODE, points), F32),
            jax.ShapeDtypeStruct((OWN, 2, NB, NB), F32),
        ),
        in_specs=[any_space, any_space, any_space, any_space],
        out_specs=(vmem, vmem),
        scratch_shapes=[
            pltpu.VMEM((steps, points), F32),
            pltpu.VMEM((1, points), F32),
            pltpu.VMEM((steps, points), BF16),
            pltpu.VMEM((steps, points), BF16),
            pltpu.VMEM((OWN, rows, steps), BF16),
            pltpu.VMEM((PACK_END, 128), F32),
            pltpu.VMEM((OWN, TM, 8, points), F32),
            pltpu.VMEM((OWN, 2, 8, points), F32),
            pltpu.VMEM((OWN, 2, 8, points), F32),
            pltpu.VMEM((OWN, TM, 8, points), F32),
            pltpu.VMEM((OWN, 64, points), BF16),
            pltpu.VMEM((OWN, 64, points), BF16),
            pltpu.VMEM((64, 64), F32),
            pltpu.VMEM((OWN, 16, 128), F32),
            pltpu.VMEM((OWN, 16, 128), F32),
            pltpu.VMEM((OWN, CHIPS, 16, 128), F32),
            dma((points // 256 + 2,)),
            dma((2,)),
            dma((5,)),
            dma((OWN,)),
            dma((OWN,)),
            dma((OWN,)),
            dma((OWN,)),
            dma((OWN,)),
        ],
        compiler_params=pltpu.CompilerParams(
            collective_id=0, has_side_effects=True, vmem_limit_bytes=52 << 20
        ),
        cost_estimate=pl.CostEstimate(flops=4 << 30, bytes_accessed=8 << 20, transcendentals=0),
        name="spod",
    )(snapshots, weights.reshape(1, points), table, pack)
    return modes, cross


def solution(mesh):
    return jax.shard_map(
        local,
        mesh=mesh,
        in_specs=(P("tm", "space"), P("space")),
        out_specs=(P("tm", None, None, "space"), P("tm", None, None, None)),
        check_vma=False,
    )
```

```python
import functools
import math

import jax
import jax.numpy as jnp
import ml_dtypes
import numpy as np
from jax import lax
from jax.experimental import pallas as pl
from jax.experimental.pallas import tpu as pltpu
from jax.sharding import PartitionSpec as P

NFFT = 256
STRIDE = 128
NFREQ = 64
NMODE = 4
NB = 31
TM = 8
OWN = NFREQ // TM
CHIPS = 16
LAG = 2
WAIT = 2
ORDER = (0, 1, 2, 3, 7, 6, 5, 4)
ORDERED = 7
CHIP_ORDER = (0, 4, 1, 8, 12, 2, 3, 5, 13, 9, 7, 6, 15, 11, 14, 10)
MESH = pl.DeviceIdType.MESH
F32 = jnp.float32
BF16 = jnp.bfloat16
HIGHEST = lax.Precision.HIGHEST
NN = (((1,), (0,)), ((), ()))
NT = (((1,), (1,)), ((), ()))


def row_plan():
    rows = []
    for d in range(TM):
        if d <= 3:
            rows.append((d, "close"))
        elif d == 4:
            rows.append((0, "open"))
        else:
            rows.append((d, "open"))
        rows.extend((d, j) for j in range(3))
    rows.extend((d, "open") for d in (1, 2, 3, 4))
    rows.extend((d, "close") for d in (7, 6, 5, 4))
    return rows


def tables(strides):
    steps = np.arange(NFFT)
    window = 0.5 - 0.5 * np.cos(2.0 * np.pi * steps / NFFT)
    angle = 2.0 * np.pi * ((steps[None, :] * np.arange(NFREQ)[:, None]) % NFFT) / NFFT
    norm = math.sqrt(3.0 * NFFT / 8.0)
    wave = np.stack([window * np.cos(angle) / norm, -window * np.sin(angle) / norm], axis=1)
    plan = row_plan()
    full = np.zeros((TM, OWN, 2 * len(plan), strides * STRIDE), np.float32)
    for me in range(TM):
        for place, (d, kind) in enumerate(plan):
            owner = (me + d) % TM
            part = wave[owner * OWN : (owner + 1) * OWN]
            row = full[me, :, 2 * place : 2 * place + 2]
            if kind == "close":
                row[:, :, :STRIDE] = part[:, :, STRIDE:]
            elif kind == "open":
                row[:, :, (strides - 1) * STRIDE :] = part[:, :, :STRIDE]
            else:
                row[:, :, kind * STRIDE : kind * STRIDE + NFFT] = part
    high = full.astype(ml_dtypes.bfloat16)
    low = (full - high.astype(np.float32)).astype(ml_dtypes.bfloat16)
    return np.concatenate([high, low], axis=2)


def block_order(me):
    order = []
    for slot in range(TM):
        source = me + slot
        if slot == 4:
            order.append(4 * me + 3)
        elif slot in (1, 2, 3):
            order.append(4 * source + 3)
        else:
            order.append(4 * source - 1)
        order.extend(4 * source + j for j in range(3))
    return [b % (NB + 1) for b in order]


PACK_V0, PACK_COL, PACK_ROW, PACK_END = 0, 8, 72, 104
PACK_WIDE = 2048


def small_tables():
    pack = np.zeros((TM, PACK_END, PACK_WIDE), np.float32)
    b = np.arange(NB)
    m = np.arange(NMODE)
    basis = np.cos(np.pi * (b[:, None] + 0.5) * m[None, :] / NB)
    for me in range(TM):
        for place, block in enumerate(block_order(me)):
            if block < NB:
                pack[me, PACK_V0 : PACK_V0 + 4, 2 * place] = basis[block]
                pack[me, PACK_V0 + 4 : PACK_V0 + 8, 2 * place + 1] = basis[block]
            pack[me, PACK_COL + 2 * place, block] = 1.0
            pack[me, PACK_COL + 2 * place + 1, 32 + block] = 1.0
            pack[me, PACK_ROW + block, place] = 1.0
    return pack


def split(value):
    high = value.astype(BF16)
    return high, (value - high.astype(F32)).astype(BF16)


def dot3(a, b, dims=NN):
    ah, al = split(a)
    bh, bl = split(b)
    return dot(ah, bh, dims) + (dot(ah, bl, dims) + dot(al, bh, dims))


def dot(a, b, dims=NN, precision=None):
    return lax.dot_general(a, b, dims, precision=precision, preferred_element_type=F32)


def kernel(
    x_hbm, w_hbm, table_hbm, pack_hbm, modes_ref, cross_ref,
    x, w_ref, xh, xl, table, pack, made, halo_out, halo_in, got, ah, al, gram, core_out, core_in, chip_all,
    load_sem, table_sem, send_sem, halo_rsem, tile_rsem, far_rsem, core_rsem, chip_rsem,
):
    points = x.shape[1]
    me = lax.axis_index("tm")
    space = lax.axis_index("space")
    core = lax.rem(space, 2)
    chip = space // 2
    cx = chip // 4
    cy = lax.rem(chip, 4)

    def along(d):
        return (lax.rem(me + d + TM, TM), space)

    others = [(i, j) for i in range(4) for j in range(4) if i or j]
    others.sort(key=lambda ij: -(min(ij[0], 4 - ij[0]) + min(ij[1], 4 - ij[1])))

    def chip_of(i, j):
        return lax.rem(cx + i, 4) * 4 + lax.rem(cy + j, 4)

    def across(i, j):
        return (me, chip_of(i, j) * 2 + core)

    mate = (me, chip * 2 + 1 - core)

    pieces = points // 256

    def load_x(p):
        columns = pl.ds(p * 256, 256)
        return pltpu.make_async_copy(x_hbm.at[:, columns], x.at[:, columns], load_sem.at[p])

    def load_pack():
        return pltpu.make_async_copy(
            pack_hbm.at[me, :, pl.ds(0, 128)], pack, load_sem.at[pieces]
        )

    def load_w():
        return pltpu.make_async_copy(w_hbm, w_ref, load_sem.at[pieces + 1])

    def load_table():
        return pltpu.make_async_copy(table_hbm.at[me, 0], table.at[0], table_sem.at[0])

    def load_tables():
        rest = pl.ds(1, OWN - 1)
        return pltpu.make_async_copy(table_hbm.at[me, rest], table.at[rest], table_sem.at[1])

    load_table().start()
    for p in range(pieces):
        load_x(p).start()
    load_pack().start()
    load_w().start()
    load_tables().start()
    barrier = pltpu.get_barrier_semaphore()
    for d in range(1, TM):
        pl.semaphore_signal(barrier, inc=1, device_id=along(d), device_id_type=MESH)
    for i, j in others:
        pl.semaphore_signal(barrier, inc=1, device_id=across(i, j), device_id_type=MESH)
    pl.semaphore_signal(barrier, inc=1, device_id=mate, device_id_type=MESH)


    def halo_copy(c, side):
        return pltpu.make_async_remote_copy(
            src_ref=halo_out.at[c, side], dst_ref=halo_in.at[c, side],
            send_sem=send_sem.at[0], recv_sem=halo_rsem.at[c],
            device_id=along(1 if side == 0 else -1), device_id_type=MESH,
        )

    def tile_copy(c, d):
        slot = lax.rem(TM - d, TM)
        return pltpu.make_async_remote_copy(
            src_ref=made.at[c, d], dst_ref=got.at[c, slot],
            send_sem=send_sem.at[1], recv_sem=tile_rsem.at[c],
            device_id=along(d), device_id_type=MESH,
        )

    def far_copy(c):
        rows = pl.ds(2, 6)
        return pltpu.make_async_remote_copy(
            src_ref=made.at[c, 4, rows], dst_ref=got.at[c, 4, rows],
            send_sem=send_sem.at[2], recv_sem=far_rsem.at[c],
            device_id=along(4), device_id_type=MESH,
        )

    def core_copy(c):
        return pltpu.make_async_remote_copy(
            src_ref=core_out.at[c], dst_ref=core_in.at[c],
            send_sem=send_sem.at[3], recv_sem=core_rsem.at[c],
            device_id=mate, device_id_type=MESH,
        )

    def chip_copy(c, target):
        return pltpu.make_async_remote_copy(
            src_ref=chip_all.at[c, chip], dst_ref=chip_all.at[c, chip],
            send_sem=send_sem.at[4], recv_sem=chip_rsem.at[c],
            device_id=(me, target * 2 + core), device_id_type=MESH,
        )

    def whole(ref, kind, sem):
        return pltpu.make_async_remote_copy(
            src_ref=ref, dst_ref=ref, send_sem=send_sem.at[kind], recv_sem=sem,
            device_id=mate, device_id_type=MESH,
        )

    def make(c, opening=False):
        if opening:
            load_table().wait()
        for n in range(pieces):
            columns = pl.ds(n * 256, 256)
            if opening:
                load_x(n).wait()
                high, low = split(x[:, columns])
                xh[:, columns] = high
                xl[:, columns] = low
            both = dot(table[c], xh[:, columns])
            value = both[:80] + both[80:] + dot(table[c, :80, :], xl[:, columns])
            for d in range(TM):
                made[c, d, :, columns] = value[8 * d : 8 * d + 8]
            halo_out[c, 0, :, columns] = value[64:72]
            halo_out[c, 1, :, columns] = value[72:80]

    def send_first(c):
        halo_copy(c, 0).start()
        halo_copy(c, 1).start()

        @pl.when(c < ORDERED)
        def _():
            far_copy(c).start()

    def send_rest(c):
        whole(halo_in.at[c], 0, halo_rsem.at[c]).wait_recv()
        first = me == 0
        last = me == TM - 1
        for d in range(4):
            total = made[c, d, 0:2, :] + halo_in[c, 0, 2 * d : 2 * d + 2, :]
            made[c, d, 0:2, :] = jnp.where(first, 0.0, total)
        for n, d in enumerate((4, 7, 6, 5)):
            total = made[c, d, 0:2, :] + halo_in[c, 1, 2 * n : 2 * n + 2, :]
            made[c, d, 0:2, :] = jnp.where(last, 0.0, total)
        @pl.when(c < ORDERED)
        def _():
            for d in (5, 3, 6, 2, 7, 1):
                tile_copy(c, d).start()

        @pl.when(c >= ORDERED)
        def _():
            for owner in ORDER:
                d = lax.rem(owner - me + TM, TM)

                @pl.when((d != 0) & (d != 4))
                def _():
                    tile_copy(c, d).start()

                @pl.when(d == 4)
                def _():
                    far_copy(c).start()

    def correlate(c):
        far_copy(c).wait_recv()
        whole(got.at[c, pl.ds(0, 6)], 1, tile_rsem.at[c]).wait_recv()
        own_rows = lax.broadcasted_iota(jnp.int32, (8, points), 0) < 2
        tiles = [made[c, 0]]
        for slot in range(1, TM):
            tile = got[c, slot]
            if slot == 4:
                tile = jnp.where(own_rows, made[c, 4], tile)
            tiles.append(tile)
        value = jnp.concatenate(tiles, axis=0)
        high, low = split(value)
        ah[c] = high
        al[c] = low
        whigh, wlow = split(value * w_ref[...])
        product = dot(high, whigh, NT) + dot(high, wlow, NT) + dot(low, whigh, NT)
        gram[...] = jnp.concatenate([product, product], axis=1)
        even = gram[pl.ds(0, 32, stride=2), :]
        odd = gram[pl.ds(1, 32, stride=2), :]
        lanes = lax.broadcasted_iota(jnp.int32, odd.shape, 1)
        turned = jnp.where(lanes % 2 == 0, pltpu.roll(odd, 127, 1), -pltpu.roll(odd, 1, 1))
        kept = (even + turned)[:, :64]
        core_out[c] = jnp.concatenate([kept[:16], kept[16:]], axis=1)
        core_copy(c).start()

    def spread(c):
        core_copy(c).wait_recv()
        chip_all[c, chip] = core_out[c] + core_in[c]
        for target in CHIP_ORDER:

            @pl.when(target != chip)
            def _():
                chip_copy(c, target).start()

    def finish(c):
        whole(chip_all.at[c, pl.ds(0, CHIPS - 1)], 4, chip_rsem.at[c]).wait_recv()
        parts = [chip_all[c, n] for n in range(CHIPS)]
        while len(parts) > 1:
            parts = [parts[n] + parts[n + 1] for n in range(0, len(parts), 2)]
        total = parts[0] / (points * 2 * CHIPS)
        total = jnp.concatenate([total, pltpu.roll(total, 64, 1)], axis=0)
        rows = lax.broadcasted_iota(jnp.int32, total.shape, 0)
        lanes = lax.broadcasted_iota(jnp.int32, total.shape, 1)
        trace = jnp.sum(jnp.where(lanes == 2 * rows, total, 0.0)) + 1e-06
        scale = NB / trace
        odd = jnp.where(lanes % 2 == 0, -pltpu.roll(total, 127, 1), pltpu.roll(total, 1, 1))
        wide = jnp.concatenate([total, odd], axis=0)[:, :64]
        one = scale * dot3(pack[PACK_V0 : PACK_V0 + 8, :64], wide, NT)
        two = scale * dot3(one, wide)
        high, low = split(two)
        built = dot(high, ah[c]) + dot(high, al[c]) + dot(low, ah[c])
        built = built / NB
        modes_ref[c, 0] = built[:NMODE]
        modes_ref[c, 1] = built[NMODE:]
        ordered = dot(total[:, :64], pack[PACK_COL : PACK_COL + 64, :], precision=HIGHEST)
        ordered = dot(pack[PACK_ROW : PACK_ROW + 32, :32], ordered, precision=HIGHEST)
        cross_ref[c, :, 0, :] = ordered[:NB, :NB]
        cross_ref[c, :, 1, :] = pltpu.roll(ordered, 96, 1)[:NB, :NB]

    make(0, opening=True)
    pl.semaphore_wait(barrier, (TM - 1) + len(others) + 1)
    send_first(0)
    load_pack().wait()
    load_w().wait()
    load_tables().wait()

    def step(s, carry):
        @pl.when(s < OWN)
        def _():
            make(s)
            send_first(s)

        @pl.when(s <= OWN)
        def _():
            send_rest(s - 1)

        @pl.when((s >= LAG) & (s < OWN + LAG))
        def _():
            correlate(s - LAG)
            spread(s - LAG)

        @pl.when(s >= LAG + WAIT)
        def _():
            finish(s - LAG - WAIT)

        return carry

    lax.fori_loop(1, OWN + LAG + WAIT, step, 0)

    whole(halo_out, 0, core_rsem.at[0]).wait_send()
    whole(made.at[:, pl.ds(0, 6)], 1, core_rsem.at[0]).wait_send()
    whole(made.at[:, 4, pl.ds(2, 6)], 2, core_rsem.at[0]).wait_send()
    whole(core_out, 3, core_rsem.at[0]).wait_send()
    whole(chip_all.at[:, pl.ds(0, CHIPS - 1)], 4, core_rsem.at[0]).wait_send()


def local(snapshots, weights):
    steps, points = snapshots.shape
    table = jnp.asarray(tables(steps // STRIDE))
    pack = jnp.asarray(small_tables())
    rows = table.shape[2]
    any_space = pl.BlockSpec(memory_space=pl.ANY)
    vmem = pl.BlockSpec(memory_space=pltpu.VMEM)
    dma = pltpu.SemaphoreType.DMA
    modes, cross = pl.pallas_call(
        kernel,
        out_shape=(
            jax.ShapeDtypeStruct((OWN, 2, NMODE, points), F32),
            jax.ShapeDtypeStruct((OWN, NB, 2, NB), F32),
        ),
        in_specs=[any_space, any_space, any_space, any_space],
        out_specs=(vmem, vmem),
        scratch_shapes=[
            pltpu.VMEM((steps, points), F32),
            pltpu.VMEM((1, points), F32),
            pltpu.VMEM((steps, points), BF16),
            pltpu.VMEM((steps, points), BF16),
            pltpu.VMEM((OWN, rows, steps), BF16),
            pltpu.VMEM((PACK_END, 128), F32),
            pltpu.VMEM((OWN, TM, 8, points), F32),
            pltpu.VMEM((OWN, 2, 8, points), F32),
            pltpu.VMEM((OWN, 2, 8, points), F32),
            pltpu.VMEM((OWN, TM, 8, points), F32),
            pltpu.VMEM((OWN, 64, points), BF16),
            pltpu.VMEM((OWN, 64, points), BF16),
            pltpu.VMEM((64, 128), F32),
            pltpu.VMEM((OWN, 16, 128), F32),
            pltpu.VMEM((OWN, 16, 128), F32),
            pltpu.VMEM((OWN, CHIPS, 16, 128), F32),
            dma((points // 256 + 2,)),
            dma((2,)),
            dma((5,)),
            dma((OWN,)),
            dma((OWN,)),
            dma((OWN,)),
            dma((OWN,)),
            dma((OWN,)),
        ],
        compiler_params=pltpu.CompilerParams(
            collective_id=0, has_side_effects=True, vmem_limit_bytes=52 << 20
        ),
        cost_estimate=pl.CostEstimate(flops=4 << 30, bytes_accessed=8 << 20, transcendentals=0),
        name="spod",
    )(snapshots, weights.reshape(1, points), table, pack)
    return modes, cross.transpose(0, 2, 1, 3)


def solution(mesh):
    return jax.shard_map(
        local,
        mesh=mesh,
        in_specs=(P("tm", "space"), P("space")),
        out_specs=(P("tm", None, None, "space"), P("tm", None, None, None)),
        check_vma=False,
    )
```

```python
import functools
import math

import jax
import jax.numpy as jnp
import ml_dtypes
import numpy as np
from jax import lax
from jax.experimental import pallas as pl
from jax.experimental.pallas import tpu as pltpu
from jax.sharding import PartitionSpec as P

NFFT = 256
STRIDE = 128
NFREQ = 64
NMODE = 4
NB = 31
TM = 8
OWN = NFREQ // TM
CHIPS = 16
LAG = 2
WAIT = 2
ORDER = (0, 1, 2, 3, 7, 6, 5, 4)
ORDERED = 7
CHIP_ORDER = (0, 4, 1, 8, 12, 2, 3, 5, 13, 9, 7, 6, 15, 11, 14, 10)
MESH = pl.DeviceIdType.MESH
F32 = jnp.float32
BF16 = jnp.bfloat16
HIGHEST = lax.Precision.HIGHEST
NN = (((1,), (0,)), ((), ()))
NT = (((1,), (1,)), ((), ()))


def row_plan():
    rows = []
    for d in range(TM):
        if d <= 3:
            rows.append((d, "close"))
        elif d == 4:
            rows.append((0, "open"))
        else:
            rows.append((d, "open"))
        rows.extend((d, j) for j in range(3))
    rows.extend((d, "open") for d in (1, 2, 3, 4))
    rows.extend((d, "close") for d in (7, 6, 5, 4))
    return rows


def tables(strides):
    steps = np.arange(NFFT)
    window = 0.5 - 0.5 * np.cos(2.0 * np.pi * steps / NFFT)
    angle = 2.0 * np.pi * ((steps[None, :] * np.arange(NFREQ)[:, None]) % NFFT) / NFFT
    norm = math.sqrt(3.0 * NFFT / 8.0)
    wave = np.stack([window * np.cos(angle) / norm, -window * np.sin(angle) / norm], axis=1)
    plan = row_plan()
    full = np.zeros((TM, OWN, 2 * len(plan), strides * STRIDE), np.float32)
    for me in range(TM):
        for place, (d, kind) in enumerate(plan):
            owner = (me + d) % TM
            part = wave[owner * OWN : (owner + 1) * OWN]
            row = full[me, :, 2 * place : 2 * place + 2]
            if kind == "close":
                row[:, :, :STRIDE] = part[:, :, STRIDE:]
            elif kind == "open":
                row[:, :, (strides - 1) * STRIDE :] = part[:, :, :STRIDE]
            else:
                row[:, :, kind * STRIDE : kind * STRIDE + NFFT] = part
    high = full.astype(ml_dtypes.bfloat16)
    low = (full - high.astype(np.float32)).astype(ml_dtypes.bfloat16)
    return np.concatenate([high, low], axis=2)


def block_order(me):
    order = []
    for slot in range(TM):
        source = me + slot
        if slot == 4:
            order.append(4 * me + 3)
        elif slot in (1, 2, 3):
            order.append(4 * source + 3)
        else:
            order.append(4 * source - 1)
        order.extend(4 * source + j for j in range(3))
    return [b % (NB + 1) for b in order]


PACK_V0, PACK_COL, PACK_ROW, PACK_END = 0, 8, 72, 104
PACK_WIDE = 2048


def small_tables():
    pack = np.zeros((TM, PACK_END, PACK_WIDE), np.float32)
    b = np.arange(NB)
    m = np.arange(NMODE)
    basis = np.cos(np.pi * (b[:, None] + 0.5) * m[None, :] / NB)
    for me in range(TM):
        for place, block in enumerate(block_order(me)):
            if block < NB:
                pack[me, PACK_V0 : PACK_V0 + 4, 2 * place] = basis[block]
                pack[me, PACK_V0 + 4 : PACK_V0 + 8, 2 * place + 1] = basis[block]
            pack[me, PACK_COL + 2 * place, block] = 1.0
            pack[me, PACK_COL + 2 * place + 1, 32 + block] = 1.0
            pack[me, PACK_ROW + block, place] = 1.0
    return pack


def split(value):
    high = value.astype(BF16)
    return high, (value - high.astype(F32)).astype(BF16)


def dot3(a, b, dims=NN):
    ah, al = split(a)
    bh, bl = split(b)
    return dot(ah, bh, dims) + (dot(ah, bl, dims) + dot(al, bh, dims))


def dot(a, b, dims=NN, precision=None):
    return lax.dot_general(a, b, dims, precision=precision, preferred_element_type=F32)


def kernel(
    x_hbm, w_hbm, table_hbm, pack_hbm, modes_ref, cross_ref,
    x, w_ref, xh, xl, table, pack, made, halo_out, halo_in, got, ah, al, gram, core_out, core_in, chip_all,
    load_sem, table_sem, send_sem, halo_rsem, tile_rsem, far_rsem, core_rsem, chip_rsem,
):
    points = x.shape[1]
    me = lax.axis_index("tm")
    space = lax.axis_index("space")
    core = lax.rem(space, 2)
    chip = space // 2
    cx = chip // 4
    cy = lax.rem(chip, 4)

    def along(d):
        return (lax.rem(me + d + TM, TM), space)

    others = [(i, j) for i in range(4) for j in range(4) if i or j]
    others.sort(key=lambda ij: -(min(ij[0], 4 - ij[0]) + min(ij[1], 4 - ij[1])))

    def chip_of(i, j):
        return lax.rem(cx + i, 4) * 4 + lax.rem(cy + j, 4)

    def across(i, j):
        return (me, chip_of(i, j) * 2 + core)

    mate = (me, chip * 2 + 1 - core)

    pieces = points // 256

    def load_x(p):
        columns = pl.ds(p * 256, 256)
        return pltpu.make_async_copy(x_hbm.at[:, columns], x.at[:, columns], load_sem.at[p])

    def load_pack():
        return pltpu.make_async_copy(
            pack_hbm.at[me, :, pl.ds(0, 128)], pack, load_sem.at[pieces]
        )

    def load_w():
        return pltpu.make_async_copy(w_hbm, w_ref, load_sem.at[pieces + 1])

    def load_table():
        return pltpu.make_async_copy(table_hbm.at[me, 0], table.at[0], table_sem.at[0])

    def load_tables():
        rest = pl.ds(1, OWN - 1)
        return pltpu.make_async_copy(table_hbm.at[me, rest], table.at[rest], table_sem.at[1])

    load_table().start()
    for p in range(pieces):
        load_x(p).start()
    load_pack().start()
    load_w().start()
    load_tables().start()
    barrier = pltpu.get_barrier_semaphore()
    for d in (4, 3, 5, 2, 6, 1, 7):
        pl.semaphore_signal(barrier, inc=1, device_id=along(d), device_id_type=MESH)
    for i, j in others:
        pl.semaphore_signal(barrier, inc=1, device_id=across(i, j), device_id_type=MESH)
    pl.semaphore_signal(barrier, inc=1, device_id=mate, device_id_type=MESH)


    def halo_copy(c, side):
        return pltpu.make_async_remote_copy(
            src_ref=halo_out.at[c, side], dst_ref=halo_in.at[c, side],
            send_sem=send_sem.at[0], recv_sem=halo_rsem.at[c],
            device_id=along(1 if side == 0 else -1), device_id_type=MESH,
        )

    def tile_copy(c, d):
        slot = lax.rem(TM - d, TM)
        return pltpu.make_async_remote_copy(
            src_ref=made.at[c, d], dst_ref=got.at[c, slot],
            send_sem=send_sem.at[1], recv_sem=tile_rsem.at[c],
            device_id=along(d), device_id_type=MESH,
        )

    def far_copy(c):
        rows = pl.ds(2, 6)
        return pltpu.make_async_remote_copy(
            src_ref=made.at[c, 4, rows], dst_ref=got.at[c, 4, rows],
            send_sem=send_sem.at[2], recv_sem=far_rsem.at[c],
            device_id=along(4), device_id_type=MESH,
        )

    def core_copy(c):
        return pltpu.make_async_remote_copy(
            src_ref=core_out.at[c], dst_ref=core_in.at[c],
            send_sem=send_sem.at[3], recv_sem=core_rsem.at[c],
            device_id=mate, device_id_type=MESH,
        )

    def chip_copy(c, target):
        return pltpu.make_async_remote_copy(
            src_ref=chip_all.at[c, chip], dst_ref=chip_all.at[c, chip],
            send_sem=send_sem.at[4], recv_sem=chip_rsem.at[c],
            device_id=(me, target * 2 + core), device_id_type=MESH,
        )

    def whole(ref, kind, sem):
        return pltpu.make_async_remote_copy(
            src_ref=ref, dst_ref=ref, send_sem=send_sem.at[kind], recv_sem=sem,
            device_id=mate, device_id_type=MESH,
        )

    def make(c, opening=False):
        if opening:
            load_table().wait()
        for n in range(pieces):
            columns = pl.ds(n * 256, 256)
            if opening:
                load_x(n).wait()
                high, low = split(x[:, columns])
                xh[:, columns] = high
                xl[:, columns] = low
            both = dot(table[c], xh[:, columns])
            value = both[:80] + both[80:] + dot(table[c, :80, :], xl[:, columns])
            for d in range(TM):
                made[c, d, :, columns] = value[8 * d : 8 * d + 8]
            halo_out[c, 0, :, columns] = value[64:72]
            halo_out[c, 1, :, columns] = value[72:80]

    def send_first(c):
        halo_copy(c, 0).start()
        halo_copy(c, 1).start()

        @pl.when(c < ORDERED)
        def _():
            far_copy(c).start()

    def send_rest(c):
        whole(halo_in.at[c], 0, halo_rsem.at[c]).wait_recv()
        first = me == 0
        last = me == TM - 1
        for d in range(4):
            total = made[c, d, 0:2, :] + halo_in[c, 0, 2 * d : 2 * d + 2, :]
            made[c, d, 0:2, :] = jnp.where(first, 0.0, total)
        for n, d in enumerate((4, 7, 6, 5)):
            total = made[c, d, 0:2, :] + halo_in[c, 1, 2 * n : 2 * n + 2, :]
            made[c, d, 0:2, :] = jnp.where(last, 0.0, total)
        @pl.when(c < ORDERED)
        def _():
            for d in (5, 3, 6, 2, 7, 1):
                tile_copy(c, d).start()

        @pl.when(c >= ORDERED)
        def _():
            for owner in ORDER:
                d = lax.rem(owner - me + TM, TM)

                @pl.when((d != 0) & (d != 4))
                def _():
                    tile_copy(c, d).start()

                @pl.when(d == 4)
                def _():
                    far_copy(c).start()

    def correlate(c):
        far_copy(c).wait_recv()
        whole(got.at[c, pl.ds(0, 6)], 1, tile_rsem.at[c]).wait_recv()
        own_rows = lax.broadcasted_iota(jnp.int32, (8, points), 0) < 2
        tiles = [made[c, 0]]
        for slot in range(1, TM):
            tile = got[c, slot]
            if slot == 4:
                tile = jnp.where(own_rows, made[c, 4], tile)
            tiles.append(tile)
        value = jnp.concatenate(tiles, axis=0)
        high, low = split(value)
        ah[c] = high
        al[c] = low
        whigh, wlow = split(value * w_ref[...])
        both = dot(jnp.concatenate([high, low], axis=0), whigh, NT)
        product = both[:64] + both[64:] + dot(high, wlow, NT)
        gram[...] = jnp.concatenate([product, product], axis=1)
        even = gram[pl.ds(0, 32, stride=2), :]
        odd = gram[pl.ds(1, 32, stride=2), :]
        lanes = lax.broadcasted_iota(jnp.int32, odd.shape, 1)
        turned = jnp.where(lanes % 2 == 0, pltpu.roll(odd, 127, 1), -pltpu.roll(odd, 1, 1))
        kept = (even + turned)[:, :64]
        core_out[c] = jnp.concatenate([kept[:16], kept[16:]], axis=1)
        core_copy(c).start()

    def spread(c):
        core_copy(c).wait_recv()
        chip_all[c, chip] = core_out[c] + core_in[c]
        for target in CHIP_ORDER:

            @pl.when(target != chip)
            def _():
                chip_copy(c, target).start()

    def finish(c):
        whole(chip_all.at[c, pl.ds(0, CHIPS - 1)], 4, chip_rsem.at[c]).wait_recv()
        parts = [chip_all[c, n] for n in range(CHIPS)]
        while len(parts) > 1:
            parts = [parts[n] + parts[n + 1] for n in range(0, len(parts), 2)]
        total = parts[0] / (points * 2 * CHIPS)
        total = jnp.concatenate([total, pltpu.roll(total, 64, 1)], axis=0)
        rows = lax.broadcasted_iota(jnp.int32, total.shape, 0)
        lanes = lax.broadcasted_iota(jnp.int32, total.shape, 1)
        trace = jnp.sum(jnp.where(lanes == 2 * rows, total, 0.0)) + 1e-06
        scale = NB / trace
        odd = jnp.where(lanes % 2 == 0, -pltpu.roll(total, 127, 1), pltpu.roll(total, 1, 1))
        wide = jnp.concatenate([total, odd], axis=0)[:, :64]
        one = scale * dot3(pack[PACK_V0 : PACK_V0 + 8, :64], wide, NT)
        two = scale * dot3(one, wide)
        high, low = split(two)
        built = dot(high, ah[c]) + dot(high, al[c]) + dot(low, ah[c])
        built = built / NB
        modes_ref[c, 0] = built[:NMODE]
        modes_ref[c, 1] = built[NMODE:]
        ordered = dot(total[:, :64], pack[PACK_COL : PACK_COL + 64, :], precision=HIGHEST)
        ordered = dot(pack[PACK_ROW : PACK_ROW + 32, :32], ordered, precision=HIGHEST)
        cross_ref[c, :, 0, :] = ordered[:NB, :NB]
        cross_ref[c, :, 1, :] = pltpu.roll(ordered, 96, 1)[:NB, :NB]

    make(0, opening=True)
    pl.semaphore_wait(barrier, (TM - 1) + len(others) + 1)
    send_first(0)
    load_pack().wait()
    load_w().wait()
    load_tables().wait()

    def step(s, carry):
        @pl.when(s < OWN)
        def _():
            make(s)
            send_first(s)

        @pl.when(s <= OWN)
        def _():
            send_rest(s - 1)

        @pl.when((s >= LAG) & (s < OWN + LAG))
        def _():
            correlate(s - LAG)
            spread(s - LAG)

        @pl.when(s >= LAG + WAIT)
        def _():
            finish(s - LAG - WAIT)

        return carry

    lax.fori_loop(1, OWN + LAG + WAIT, step, 0)

    whole(halo_out, 0, core_rsem.at[0]).wait_send()
    whole(made.at[:, pl.ds(0, 6)], 1, core_rsem.at[0]).wait_send()
    whole(made.at[:, 4, pl.ds(2, 6)], 2, core_rsem.at[0]).wait_send()
    whole(core_out, 3, core_rsem.at[0]).wait_send()
    whole(chip_all.at[:, pl.ds(0, CHIPS - 1)], 4, core_rsem.at[0]).wait_send()


def local(snapshots, weights):
    steps, points = snapshots.shape
    table = jnp.asarray(tables(steps // STRIDE))
    pack = jnp.asarray(small_tables())
    rows = table.shape[2]
    any_space = pl.BlockSpec(memory_space=pl.ANY)
    vmem = pl.BlockSpec(memory_space=pltpu.VMEM)
    dma = pltpu.SemaphoreType.DMA
    modes, cross = pl.pallas_call(
        kernel,
        out_shape=(
            jax.ShapeDtypeStruct((OWN, 2, NMODE, points), F32),
            jax.ShapeDtypeStruct((OWN, NB, 2, NB), F32),
        ),
        in_specs=[any_space, any_space, any_space, any_space],
        out_specs=(vmem, vmem),
        scratch_shapes=[
            pltpu.VMEM((steps, points), F32),
            pltpu.VMEM((1, points), F32),
            pltpu.VMEM((steps, points), BF16),
            pltpu.VMEM((steps, points), BF16),
            pltpu.VMEM((OWN, rows, steps), BF16),
            pltpu.VMEM((PACK_END, 128), F32),
            pltpu.VMEM((OWN, TM, 8, points), F32),
            pltpu.VMEM((OWN, 2, 8, points), F32),
            pltpu.VMEM((OWN, 2, 8, points), F32),
            pltpu.VMEM((OWN, TM, 8, points), F32),
            pltpu.VMEM((OWN, 64, points), BF16),
            pltpu.VMEM((OWN, 64, points), BF16),
            pltpu.VMEM((64, 128), F32),
            pltpu.VMEM((OWN, 16, 128), F32),
            pltpu.VMEM((OWN, 16, 128), F32),
            pltpu.VMEM((OWN, CHIPS, 16, 128), F32),
            dma((points // 256 + 2,)),
            dma((2,)),
            dma((5,)),
            dma((OWN,)),
            dma((OWN,)),
            dma((OWN,)),
            dma((OWN,)),
            dma((OWN,)),
        ],
        compiler_params=pltpu.CompilerParams(
            collective_id=0, has_side_effects=True, vmem_limit_bytes=52 << 20
        ),
        cost_estimate=pl.CostEstimate(flops=4 << 30, bytes_accessed=8 << 20, transcendentals=0),
        name="spod",
    )(snapshots, weights.reshape(1, points), table, pack)
    return modes, cross.transpose(0, 2, 1, 3)


def solution(mesh):
    return jax.shard_map(
        local,
        mesh=mesh,
        in_specs=(P("tm", "space"), P("space")),
        out_specs=(P("tm", None, None, "space"), P("tm", None, None, None)),
        check_vma=False,
    )
```
